768 devices in a mesh: blk: 96 (over y, x, z_lo), grp: 8 (over z_hi, core).
Axes of the slice: x: 4, y: 8, z: 12 (z_hi: 4, z_lo: 3; z = z_hi * 3 + z_lo), core: 2. Of those that a mesh axis runs over, the one named last changes fastest.
Arguments:
- images: bfloat16 [1536, 3, 1024], P(('blk', 'grp')), may hold values from -10 to 10
Outputs:
- kernel_window: float32 [1536, 5, 16], P(('blk', 'grp'))
The draws below stay inside these ranges and needn't reach their ends.
All inputs are finite; a program needn't handle non-finite values.
Results may differ from the reference program's by a relative error of at most 0.0003.
Values may be sent and summed in bfloat16 or wider, within the bound.
No kernel may reach another device: no remote copies, remote signals or barrier semaphores. Data moves between devices by JAX's collectives and lax.ppermute only.
A program may use at most 32 MiB of HBM per device.

```python
import math
import jax
import jax.numpy as jnp
from jax import lax

SIDE = 32
PIX = 1024
CHAN = 3
LAYERS = 3
ROUNDS = 2
BLOCK = 16
IMAGES = 1536
SPAN = 5
N_BLK = 96


class_total = 10


def smooth_wave(key, lead_shape):
    subkeys = jax.random.split(key, 4)
    freq_rows = jax.random.uniform(subkeys[0], lead_shape + (1,), minval=0.0, maxval=3.0)
    phase_rows = jax.random.uniform(subkeys[1], lead_shape + (1,), minval=-math.pi, maxval=math.pi)
    freq_cols = jax.random.uniform(subkeys[2], lead_shape + (1,), minval=0.0, maxval=3.0)
    phase_cols = jax.random.uniform(subkeys[3], lead_shape + (1,), minval=-math.pi, maxval=math.pi)
    pixel_index = jnp.arange(PIX)
    row_pos = (pixel_index // SIDE).astype(jnp.float32) / SIDE
    col_pos = (pixel_index % SIDE).astype(jnp.float32) / SIDE
    return jnp.cos(math.pi * freq_rows * row_pos + phase_rows) * jnp.cos(math.pi * freq_cols * col_pos + phase_cols)


def draw_images(key, part):
    key = jax.random.fold_in(key, 11)
    subkeys = jax.random.split(key, 8)
    shared = 0.8 + 0.15 * smooth_wave(subkeys[0], (CHAN,)) + 0.15 * smooth_wave(subkeys[1], (CHAN,))
    class_fields = 0.35 * smooth_wave(subkeys[2], (class_total, CHAN)) + 0.35 * smooth_wave(subkeys[3], (class_total, CHAN))
    labels = jax.random.randint(subkeys[4], (IMAGES,), 0, class_total)
    signal = shared[None, :, :] + jnp.take(class_fields, labels, axis=0)
    noise_level = jnp.exp(jax.random.uniform(subkeys[5], (IMAGES, 1, 1), minval=math.log(0.1), maxval=math.log(2.5)))
    gains = jax.random.uniform(subkeys[6], (IMAGES, 1, 1), minval=0.7, maxval=1.3)
    noise = jnp.clip(jax.random.normal(subkeys[7], (IMAGES, CHAN, PIX)), -3.0, 3.0)
    return (gains * signal + noise_level * noise).astype(jnp.bfloat16)


def setup_inputs(seed: int = 0) -> dict:
    seeds = jax.random.split(jax.random.key(seed), 2)
    return {
        "images": draw_images(jax.random.fold_in(seeds[1], 71), 0),
    }


bias_var = 0.1

def stencil_band(side):
    positions = jnp.arange(side)
    return (jnp.abs(positions[:, None] - positions[None, :]) <= 1).astype(jnp.float32)

def stencil_maps(pair_maps, band_matrix):
    shaped = pair_maps.reshape(pair_maps.shape[:-1] + (SIDE, SIDE))
    first = jnp.einsum('ab,...bc->...ac', band_matrix, shaped, precision=lax.Precision.HIGHEST)
    second = jnp.einsum('...ac,dc->...ad', first, band_matrix, precision=lax.Precision.HIGHEST)
    return (second / 9.0).reshape(pair_maps.shape)

def variance_maps(image_data, band_matrix):
    current = stencil_maps(lax.optimization_barrier(jnp.mean(image_data * image_data, axis=1)), band_matrix) + bias_var
    layers_out = [current]
    for layer in range(LAYERS - 1):
        current = stencil_maps(current, band_matrix) + bias_var
        layers_out.append(current)
    return jnp.stack(layers_out, 0)

def relu_expect(cov_map, var_left, var_right):
    scale_root = jnp.sqrt(var_left * var_right)
    ratio = jnp.clip(cov_map / scale_root, -1.0, 1.0)
    angle_map = jnp.arccos(ratio)
    return scale_root * (jnp.sqrt(1.0 - ratio * ratio) + (jnp.pi - angle_map) * ratio) / (2.0 * jnp.pi)

def pair_kernel(left_img, right_img, left_var, right_var, band_matrix):
    product = jnp.einsum('acp,bcp->abp', left_img, right_img, preferred_element_type=jnp.float32) / left_img.shape[1]
    cov_map = stencil_maps(product, band_matrix) + bias_var
    expect = cov_map
    for layer in range(LAYERS):
        expect = relu_expect(cov_map, left_var[layer][:, None, :], right_var[layer][None, :, :])
        if layer < LAYERS - 1:
            cov_map = 2.0 * stencil_maps(expect, band_matrix) + bias_var
    return lax.optimization_barrier(jnp.mean(2.0 * expect, axis=-1))

def reference(images):
    band_matrix = stencil_band(SIDE)
    image_data = images.astype(jnp.float32)
    all_var = variance_maps(image_data, band_matrix)
    blocked = images.reshape(N_BLK, BLOCK, CHAN, PIX)
    blocked_var = all_var.reshape(LAYERS, N_BLK, BLOCK, PIX)

    def one_block(block_index):
        rows_img = blocked[block_index]
        rows_var = blocked_var[:, block_index]
        kernel_tiles = []
        for offset in range(-ROUNDS, ROUNDS + 1):
            other = ((block_index + offset + N_BLK) % N_BLK).astype(jnp.int32)
            kernel_tiles.append(pair_kernel(rows_img, blocked[other], rows_var, blocked_var[:, other], band_matrix))
        return jnp.stack(kernel_tiles, 1)
    result = lax.map(one_block, jnp.arange(N_BLK).astype(jnp.int32))
    return result.reshape(IMAGES, SPAN, BLOCK)
```

```python
import functools

import jax
import jax.numpy as jnp
import numpy as np
from jax import lax
from jax.experimental import pallas as pl
from jax.experimental.pallas import tpu as pltpu
from jax.sharding import PartitionSpec as P

SIDE = 32
LAYERS = 3
CHIP_ROWS = 4
GRP = 8
bias_var = 0.1

TAIL = (
    0.3001054023535799,
    0.015007729426877447,
    0.0023848543747712397,
    0.0006623160561359935,
    -2.0047167192458316e-05,
    0.00016959256815365074,
)


def stencil_weights():
    lane = np.arange(128)
    row, col = lane // SIDE, lane % SIDE
    near = np.abs(col[:, None] - col[None, :]) <= 1
    inner = near & (np.abs(row[:, None] - row[None, :]) <= 1)
    cross = near & (
        ((row[:, None] == 3) & (row[None, :] == 0)) | ((row[:, None] == 0) & (row[None, :] == 3))
    )
    half = np.concatenate([inner, cross], 1).astype(np.float32)
    return np.concatenate([half, half], 0)


def split(x):
    high = x.astype(jnp.bfloat16)
    low = (x - high.astype(jnp.float32)).astype(jnp.bfloat16)
    return high, low


def stencil_sum(maps, weights, from_above, from_below):
    count = maps.shape[0]
    high, low = split(maps.reshape(count * 8, 128))
    both = jnp.dot(
        jnp.concatenate([high, low], 1), weights, preferred_element_type=jnp.float32
    )
    inner = both[:, :128].reshape(count, 8, 128)
    cross = both[:, 128:].reshape(count, 8, 128)
    down = pltpu.roll(cross, 1, 1)
    up = pltpu.roll(cross, 7, 1)
    return inner + jnp.where(from_above, down, jnp.where(from_below, up, 0.0))


def masks():
    sub = lax.broadcasted_iota(jnp.int32, (1, 8, 128), 1)
    lane = lax.broadcasted_iota(jnp.int32, (1, 8, 128), 2)
    return (lane < SIDE) & (sub >= 1), (lane >= 3 * SIDE) & (sub <= 6)


def load_images(ref, first, count):
    pairs = ref[pl.ds(first, count)].astype(jnp.float32)
    return pairs.reshape(count * 2, 3, 8, 128)


def variance_maps(channels, weights, above, below):
    current = jnp.sum(channels * channels, 1) * (1.0 / 27.0)
    out = []
    for layer in range(LAYERS):
        if layer:
            current = current * (1.0 / 9.0)
        current = stencil_sum(current, weights, above, below) + bias_var
        inverse = lax.rsqrt(current)
        out.append((inverse, current * inverse))
    return out


def relu_over_scale(ratio):
    gap = 1.0 - jnp.minimum(jnp.abs(ratio), 1.0)
    poly = jnp.float32(TAIL[-1])
    for coefficient in TAIL[-2::-1]:
        poly = poly * gap + jnp.float32(coefficient)
    return jnp.clip(ratio, 0.0, 1.0) + gap * gap * lax.rsqrt(jnp.maximum(gap, 1e-30)) * poly


def fold(maps):
    sub = lax.broadcasted_iota(jnp.int32, (1, 8, 128), 1)
    for width in (4, 2, 1):
        first, second = maps[:width], maps[width:]
        low = (sub % (2 * width)) < width
        kept = jnp.where(low, first, second)
        if width == 4:
            other = pltpu.roll(jnp.where(low, second, first), 4, 1)
        else:
            other = jnp.where(low, pltpu.roll(first, 8 - width, 1), pltpu.roll(second, width, 1))
        maps = kept + other
    return maps[0]


def lane_sums(rows):
    ones = jnp.ones((8, 256), jnp.bfloat16)
    return lax.dot_general(
        ones,
        jnp.concatenate(split(rows), 1),
        (((1,), (1,)), ((), ())),
        preferred_element_type=jnp.float32,
    )


def pair_tile(row_refs, columns, weights, above, below):
    count = columns.shape[0]
    column_var = variance_maps(columns, weights, above, below)
    tile = jnp.zeros((8, 128), jnp.float32)
    sub = lax.broadcasted_iota(jnp.int32, (8, 128), 0)
    for row in range(CHIP_ROWS):
        folded = []
        for group in range(0, count, 8):
            part = slice(group, group + 8)
            product = row_refs[row, 0][None] * columns[part, 0]
            for channel in (1, 2):
                product = product + row_refs[row, channel][None] * columns[part, channel]
            for layer in range(LAYERS):
                cov = stencil_sum(product, weights, above, below) + bias_var
                inverse, scale = column_var[layer]
                ratio = cov * (row_refs[row, 3 + layer][None] * inverse[part])
                product = (row_refs[row, 6 + layer][None] * scale[part]) * relu_over_scale(ratio)
            folded.append(fold(product))
        sums = lane_sums(jnp.concatenate(folded, 0))
        sums = jnp.concatenate([sums, jnp.zeros((8, 128 - count), jnp.float32)], 1)
        tile = jnp.where(sub == row, sums, tile)
    return tile


def own_kernel(block_ref, weights_ref, tile_ref, rows_ref):
    place = lax.axis_index("grp")
    chip, core = place // 2, place % 2
    weights = weights_ref[...]
    above, below = masks()
    rows = load_images(block_ref, 2 * chip, 2)
    row_var = variance_maps(rows, weights, above, below)
    for channel in range(3):
        rows_ref[:, channel] = rows[:, channel] * (1.0 / 27.0)
    for layer in range(LAYERS):
        inverse, scale = row_var[layer]
        rows_ref[:, 3 + layer] = inverse
        rows_ref[:, 6 + layer] = scale * (1.0 / 9.0 if layer < LAYERS - 1 else 1.0 / 1024.0)
    columns = load_images(block_ref, 4 * core, 4)
    tile_ref[...] = pair_tile(rows_ref, columns, weights, above, below)


def visitor_kernel(rows_ref, block_ref, weights_ref, tile_ref):
    above, below = masks()
    columns = load_images(block_ref, 0, GRP)
    tile_ref[...] = pair_tile(rows_ref, columns, weights_ref[...], above, below)


def last_kernel(rows_ref, block_ref, weights_ref, own_ref, near_ref, tile_ref):
    above, below = masks()
    columns = load_images(block_ref, 0, GRP)
    far = pair_tile(rows_ref, columns, weights_ref[...], above, below)
    tile_ref[...] = own_ref[...] + pltpu.roll(near_ref[...], 8, 1) + pltpu.roll(far, 24, 1)


def call(body, outs, pairs):
    return pl.pallas_call(
        body,
        out_shape=outs,
        compiler_params=pltpu.CompilerParams(vmem_limit_bytes=32 * 1024 * 1024),
        cost_estimate=pl.CostEstimate(
            flops=pairs * 3 * 1024 * 512, bytes_accessed=1 << 20, transcendentals=pairs * 3 * 1024
        ),
    )


def by_core(block, distance, blocks):
    route = []
    for block_index in range(blocks):
        for place in range(GRP):
            source = (block_index + (distance if place % 2 else -distance)) % blocks
            route.append((source * GRP + place, block_index * GRP + place))
    return lax.ppermute(block, ("blk", "grp"), route)


def per_device(images):
    blocks = lax.axis_size("blk")
    weights = jnp.asarray(stencil_weights(), jnp.bfloat16)
    mine = images.reshape(1, 48, 128)
    block = lax.all_gather(mine, "grp", axis=0, tiled=True)
    near = by_core(block, 1, blocks)
    far = by_core(block, 2, blocks)
    tile = jax.ShapeDtypeStruct((8, 128), jnp.float32)
    rows = jax.ShapeDtypeStruct((CHIP_ROWS, 9, 8, 128), jnp.float32)
    own_tile, row_maps = call(own_kernel, (tile, rows), 32)(block, weights)
    near_tile = call(visitor_kernel, tile, 64)(row_maps, near, weights)
    packed = call(last_kernel, tile, 64)(row_maps, far, weights, own_tile, near_tile)
    chips = [[2 * chip, 2 * chip + 1] for chip in range(GRP // 2)]
    both = lax.all_gather(packed, "grp", axis=0, axis_index_groups=chips)
    core = lax.axis_index("grp") % 2
    mine = lax.dynamic_slice(both, (0, 2 * core, 0), (2, 2, 40))
    low, high = mine[0], mine[1]
    return jnp.stack(
        [
            low[:, 24:40],
            low[:, 8:24],
            jnp.concatenate([low[:, :8], high[:, :8]], 1),
            high[:, 8:24],
            high[:, 24:40],
        ],
        1,
    )


def solution(mesh):
    in_specs = (P(("blk", "grp"), None, None),)
    out_specs = P(("blk", "grp"), None, None)
    return jax.shard_map(
        per_device, mesh=mesh, in_specs=in_specs, out_specs=out_specs, check_vma=False
    )
```

```python
import functools

import jax
import jax.numpy as jnp
import numpy as np
from jax import lax
from jax.experimental import pallas as pl
from jax.experimental.pallas import tpu as pltpu
from jax.sharding import PartitionSpec as P

SIDE = 32
LAYERS = 3
CHIP_ROWS = 4
GRP = 8
bias_var = 0.1

TAIL = (
    0.3001054023535799,
    0.015007729426877447,
    0.0023848543747712397,
    0.0006623160561359935,
    -2.0047167192458316e-05,
    0.00016959256815365074,
)


def stencil_weights():
    lane = np.arange(128)
    row, col = lane // SIDE, lane % SIDE
    near = np.abs(col[:, None] - col[None, :]) <= 1
    inner = near & (np.abs(row[:, None] - row[None, :]) <= 1)
    cross = near & (
        ((row[:, None] == 3) & (row[None, :] == 0)) | ((row[:, None] == 0) & (row[None, :] == 3))
    )
    half = np.concatenate([inner, cross], 1).astype(np.float32)
    return np.concatenate([half, half], 0)


def split(x):
    high = x.astype(jnp.bfloat16)
    low = (x - high.astype(jnp.float32)).astype(jnp.bfloat16)
    return high, low


def stencil_sum(maps, weights, from_above, from_below):
    count = maps.shape[0]
    high, low = split(maps.reshape(count * 8, 128))
    both = jnp.dot(
        jnp.concatenate([high, low], 1), weights, preferred_element_type=jnp.float32
    )
    inner = both[:, :128].reshape(count, 8, 128)
    cross = both[:, 128:].reshape(count, 8, 128)
    down = pltpu.roll(cross, 1, 1)
    up = pltpu.roll(cross, 7, 1)
    return inner + jnp.where(from_above, down, jnp.where(from_below, up, 0.0))


def masks():
    sub = lax.broadcasted_iota(jnp.int32, (1, 8, 128), 1)
    lane = lax.broadcasted_iota(jnp.int32, (1, 8, 128), 2)
    return (lane < SIDE) & (sub >= 1), (lane >= 3 * SIDE) & (sub <= 6)


def load_images(ref, places, spread, slot=0):
    images = []
    for place in places:
        spread[pl.ds(slot * 48, 48)] = ref[place].astype(jnp.float32)
        for image in range(2):
            images += [
                spread[pl.ds(slot * 48 + channel * 16 + image, 8, stride=2)]
                for channel in range(3)
            ]
        slot += 1
    return jnp.stack(images, 0).reshape(2 * len(places), 3, 8, 128)


def relu_over_scale(ratio):
    gap = 1.0 - jnp.minimum(jnp.abs(ratio), 1.0)
    poly = jnp.float32(TAIL[-1])
    for coefficient in TAIL[-2::-1]:
        poly = poly * gap + jnp.float32(coefficient)
    return jnp.clip(ratio, 0.0, 1.0) + gap * gap * lax.rsqrt(jnp.maximum(gap, 1e-30)) * poly


def fold(maps):
    sub = lax.broadcasted_iota(jnp.int32, (1, 8, 128), 1)
    for width in (4, 2, 1):
        first, second = maps[:width], maps[width:]
        low = (sub % (2 * width)) < width
        kept = jnp.where(low, first, second)
        if width == 4:
            other = pltpu.roll(jnp.where(low, second, first), 4, 1)
        else:
            other = jnp.where(low, pltpu.roll(first, 8 - width, 1), pltpu.roll(second, width, 1))
        maps = kept + other
    return maps[0]


def lane_sums(rows):
    ones = jnp.ones((8, 256), jnp.bfloat16)
    return lax.dot_general(
        ones,
        jnp.concatenate(split(rows), 1),
        (((1,), (1,)), ((), ())),
        preferred_element_type=jnp.float32,
    )


def squares(channels):
    return jnp.sum(channels * channels, 1) * (1.0 / 27.0)


def pair_tile(row_channels, columns, weights, row_maps=None):
    above, below = masks()
    count = columns.shape[0]
    pairs = CHIP_ROWS * count
    products = []
    for row in range(CHIP_ROWS):
        terms = (row_channels[row] * (1.0 / 27.0))[None] * columns
        products.append(terms[:, 0] + terms[:, 1] + terms[:, 2])
    maps = products + [squares(columns)]
    if row_maps is None:
        maps.append(squares(row_channels))
    made = []
    for layer in range(LAYERS):
        sums = stencil_sum(jnp.concatenate(maps, 0), weights, above, below) + bias_var
        variance = sums[pairs:]
        inverse = lax.rsqrt(variance)
        scale = variance * inverse
        if row_maps is None:
            factor = 1.0 / 9.0 if layer < LAYERS - 1 else 1.0 / 1024.0
            row_inverse, row_scale = inverse[count:], scale[count:] * factor
            made.append((row_inverse, row_scale))
        else:
            row_inverse, row_scale = row_maps[layer]
        maps = []
        for row in range(CHIP_ROWS):
            part = sums[row * count : (row + 1) * count]
            ratio = part * (row_inverse[row][None] * inverse[:count])
            maps.append((row_scale[row][None] * scale[:count]) * relu_over_scale(ratio))
        if layer < LAYERS - 1:
            maps.append(variance * (1.0 / 9.0))
    tile = jnp.zeros((8, 128), jnp.float32)
    sub = lax.broadcasted_iota(jnp.int32, (8, 128), 0)
    for row in range(CHIP_ROWS):
        folded = [fold(maps[row][group : group + 8]) for group in range(0, count, 8)]
        sums = lane_sums(jnp.concatenate(folded, 0))
        sums = jnp.concatenate([sums, jnp.zeros((8, 128 - count), jnp.float32)], 1)
        tile = jnp.where(sub == row, sums, tile)
    return tile, made


def own_kernel(block_ref, weights_ref, tile_ref, rows_ref, spread):
    place = lax.axis_index("grp")
    chip, core = place // 2, place % 2
    at = 2 * jnp.where(chip == 0, 0, jnp.where(chip == 1, 2, jnp.where(chip == 2, 3, 1)))
    rows = load_images(block_ref, (at, at + 1), spread)
    first, second = jnp.where(core == 0, 0, 6), jnp.where(core == 0, 4, 2)
    columns = load_images(block_ref, (first, first + 1, second, second + 1), spread, 2)
    tile, row_maps = pair_tile(rows, columns, weights_ref[...])
    tile_ref[...] = tile
    rows_ref[:, :3] = rows
    for layer in range(LAYERS):
        rows_ref[:, 3 + layer] = row_maps[layer][0]
        rows_ref[:, 6 + layer] = row_maps[layer][1]


def visitor_tile(rows_ref, block_ref, weights_ref, spread):
    columns = load_images(block_ref, (0, 1, 4, 5, 6, 7, 2, 3), spread)
    row_maps = [(rows_ref[:, 3 + layer], rows_ref[:, 6 + layer]) for layer in range(LAYERS)]
    return pair_tile(rows_ref[:, :3], columns, weights_ref[...], row_maps)[0]


def visitor_kernel(rows_ref, block_ref, weights_ref, tile_ref, spread):
    tile_ref[...] = visitor_tile(rows_ref, block_ref, weights_ref, spread)


def last_kernel(rows_ref, block_ref, weights_ref, own_ref, inside_ref, tile_ref, spread):
    cross = visitor_tile(rows_ref, block_ref, weights_ref, spread)
    tile_ref[...] = own_ref[...] + pltpu.roll(inside_ref[...], 8, 1) + pltpu.roll(cross, 24, 1)


def assemble_kernel(both_ref, out_ref):
    level = lax.axis_index("blk") % 3
    core = lax.axis_index("grp") % 2
    low, high = [jnp.where(core == 0, both_ref[at, :2], both_ref[at, 2:4]) for at in (0, 1)]
    low_inside, high_inside = low[:, 8:24], high[:, 8:24]
    low_cross, high_cross = low[:, 24:40], high[:, 24:40]
    out_ref[0] = jnp.where(level == 2, high_inside, low_cross)
    out_ref[1] = jnp.where(level == 0, high_cross, low_inside)
    out_ref[2] = jnp.concatenate([low[:, :8], high[:, :8]], 1)
    out_ref[3] = jnp.where(level == 2, low_cross, high_inside)
    out_ref[4] = jnp.where(level == 0, low_inside, high_cross)


def call(body, outs, pairs, places):
    return pl.pallas_call(
        body,
        out_shape=outs,
        scratch_shapes=[pltpu.VMEM((places * 48, 128), jnp.float32)] if places else [],
        compiler_params=pltpu.CompilerParams(vmem_limit_bytes=32 * 1024 * 1024),
        cost_estimate=pl.CostEstimate(
            flops=pairs * 3 * 1024 * 512, bytes_accessed=1 << 20, transcendentals=pairs * 3 * 1024
        ),
    )


def routes():
    lines = 32

    def device(line, level, chip, core):
        return ((line % lines) * 3 + level) * GRP + chip * 2 + core

    across = {
        (0, 0): (-1, 1),
        (0, 1): (-1, 2),
        (1, 0): (-1, 2),
        (1, 1): (1, 0),
        (2, 0): (1, 0),
        (2, 1): (1, 1),
    }
    cross, inside, used = [], [], {}
    for line in range(lines):
        for chip in range(GRP // 2):
            for level in range(3):
                for core in (0, 1):
                    here = device(line, level, chip, core)
                    step, source = across[level, core]
                    sender = (line + step) % lines, source, chip
                    turn = used.get(sender, 0)
                    used[sender] = turn + 1
                    cross.append((device(*sender, turn), here))
                    source = (level + (1 if core else 2)) % 3
                    inside.append((device(line, source, chip, 1 - core), here))
    return cross, inside


def per_device(images):
    weights = jnp.asarray(stencil_weights(), jnp.bfloat16)
    mine = images.reshape(2, 3, 8, 128).transpose(1, 2, 0, 3).reshape(1, 48, 128)
    halves = [[0, 1, 6, 7], [2, 3, 4, 5]]
    pairs = [[0, 2], [1, 3], [6, 4], [7, 5]]
    block = lax.all_gather(mine, "grp", axis=0, tiled=True, axis_index_groups=halves)
    block = lax.all_gather(block, "grp", axis=0, tiled=True, axis_index_groups=pairs)
    cross_route, inside_route = routes()
    inside = lax.ppermute(block, ("blk", "grp"), inside_route)
    cross = lax.ppermute(block, ("blk", "grp"), cross_route)
    tile = jax.ShapeDtypeStruct((8, 128), jnp.float32)
    rows = jax.ShapeDtypeStruct((CHIP_ROWS, 9, 8, 128), jnp.float32)
    own_tile, row_maps = call(own_kernel, (tile, rows), 32, 6)(block, weights)
    inside_tile = call(visitor_kernel, tile, 64, GRP)(row_maps, inside, weights)
    packed = call(last_kernel, tile, 64, GRP)(row_maps, cross, weights, own_tile, inside_tile)
    chips = [[2 * chip, 2 * chip + 1] for chip in range(GRP // 2)]
    both = lax.all_gather(packed, "grp", axis=0, axis_index_groups=chips)
    result = call(assemble_kernel, jax.ShapeDtypeStruct((5, 2, 16), jnp.float32), 0, 0)(both)
    return jnp.transpose(result, (1, 0, 2))


def solution(mesh):
    in_specs = (P(("blk", "grp"), None, None),)
    out_specs = P(("blk", "grp"), None, None)
    return jax.shard_map(
        per_device, mesh=mesh, in_specs=in_specs, out_specs=out_specs, check_vma=False
    )
```

```python
import functools

import jax
import jax.numpy as jnp
import numpy as np
from jax import lax
from jax.experimental import pallas as pl
from jax.experimental.pallas import tpu as pltpu
from jax.sharding import PartitionSpec as P

SIDE = 32
LAYERS = 3
CHIP_ROWS = 4
GRP = 8
bias_var = 0.1

ORDER = (0, 2, 4, 6, 5, 7, 1, 3)

TAIL = (
    0.3001054023535799,
    0.015007729426877447,
    0.0023848543747712397,
    0.0006623160561359935,
    -2.0047167192458316e-05,
    0.00016959256815365074,
)


def stencil_weights():
    lane = np.arange(128)
    row, col = lane // SIDE, lane % SIDE
    near = np.abs(col[:, None] - col[None, :]) <= 1
    inner = near & (np.abs(row[:, None] - row[None, :]) <= 1)
    cross = near & (
        ((row[:, None] == 3) & (row[None, :] == 0)) | ((row[:, None] == 0) & (row[None, :] == 3))
    )
    half = np.concatenate([inner, cross], 1).astype(np.float32)
    return np.concatenate([half, half], 0)


def split(x):
    high = x.astype(jnp.bfloat16)
    low = (x - high.astype(jnp.float32)).astype(jnp.bfloat16)
    return high, low


def stencil_sum(maps, weights, from_above, from_below):
    count = maps.shape[0]
    high, low = split(maps.reshape(count * 8, 128))
    both = jnp.dot(
        jnp.concatenate([high, low], 1), weights, preferred_element_type=jnp.float32
    )
    inner = both[:, :128].reshape(count, 8, 128)
    cross = both[:, 128:].reshape(count, 8, 128)
    down = pltpu.roll(cross, 1, 1)
    up = pltpu.roll(cross, 7, 1)
    return inner + jnp.where(from_above, down, jnp.where(from_below, up, 0.0))


def masks():
    sub = lax.broadcasted_iota(jnp.int32, (1, 8, 128), 1)
    lane = lax.broadcasted_iota(jnp.int32, (1, 8, 128), 2)
    return (lane < SIDE) & (sub >= 1), (lane >= 3 * SIDE) & (sub <= 6)


def load_images(ref, places, spread, slot=0):
    images = []
    for place in places:
        spread[pl.ds(slot * 48, 48)] = ref[place].astype(jnp.float32)
        for image in range(2):
            images += [
                spread[pl.ds(slot * 48 + channel * 16 + image, 8, stride=2)]
                for channel in range(3)
            ]
        slot += 1
    return jnp.stack(images, 0).reshape(2 * len(places), 3, 8, 128)


def relu_over_scale(ratio):
    gap = 1.0 - jnp.minimum(jnp.abs(ratio), 1.0)
    poly = jnp.float32(TAIL[-1])
    for coefficient in TAIL[-2::-1]:
        poly = poly * gap + jnp.float32(coefficient)
    return jnp.clip(ratio, 0.0, 1.0) + gap * gap * lax.rsqrt(jnp.maximum(gap, 1e-30)) * poly


def fold(maps):
    sub = lax.broadcasted_iota(jnp.int32, (1, 8, 128), 1)
    for width in (4, 2, 1):
        first, second = maps[:width], maps[width:]
        low = (sub % (2 * width)) < width
        kept = jnp.where(low, first, second)
        if width == 4:
            other = pltpu.roll(jnp.where(low, second, first), 4, 1)
        else:
            other = jnp.where(low, pltpu.roll(first, 8 - width, 1), pltpu.roll(second, width, 1))
        maps = kept + other
    return maps[0]


def lane_sums(rows):
    ones = jnp.ones((8, 256), jnp.bfloat16)
    return lax.dot_general(
        ones,
        jnp.concatenate(split(rows), 1),
        (((1,), (1,)), ((), ())),
        preferred_element_type=jnp.float32,
    )


def squares(channels):
    return jnp.sum(channels * channels, 1) * (1.0 / 27.0)


def pair_tile(row_channels, columns, weights, row_maps=None):
    above, below = masks()
    count = columns.shape[0]
    pairs = CHIP_ROWS * count
    products = []
    for row in range(CHIP_ROWS):
        terms = (row_channels[row] * (1.0 / 27.0))[None] * columns
        products.append(terms[:, 0] + terms[:, 1] + terms[:, 2])
    maps = products + [squares(columns)]
    if row_maps is None:
        maps.append(squares(row_channels))
    made = []
    for layer in range(LAYERS):
        sums = stencil_sum(jnp.concatenate(maps, 0), weights, above, below) + bias_var
        variance = sums[pairs:]
        inverse = lax.rsqrt(variance)
        scale = variance * inverse
        if row_maps is None:
            factor = 1.0 / 9.0 if layer < LAYERS - 1 else 1.0 / 1024.0
            row_inverse, row_scale = inverse[count:], scale[count:] * factor
            made.append((row_inverse, row_scale))
        else:
            row_inverse, row_scale = row_maps[layer]
        maps = []
        for row in range(CHIP_ROWS):
            part = sums[row * count : (row + 1) * count]
            ratio = part * (row_inverse[row][None] * inverse[:count])
            maps.append((row_scale[row][None] * scale[:count]) * relu_over_scale(ratio))
        if layer < LAYERS - 1:
            maps.append(variance * (1.0 / 9.0))
    tile = jnp.zeros((8, 128), jnp.float32)
    sub = lax.broadcasted_iota(jnp.int32, (8, 128), 0)
    for row in range(CHIP_ROWS):
        folded = [fold(maps[row][group : group + 8]) for group in range(0, count, 8)]
        sums = lane_sums(jnp.concatenate(folded, 0))
        sums = jnp.concatenate([sums, jnp.zeros((8, 128 - count), jnp.float32)], 1)
        tile = jnp.where(sub == row, sums, tile)
    return tile, made


def own_kernel(block_ref, weights_ref, tile_ref, rows_ref, spread):
    place = lax.axis_index("grp")
    chip, core = place // 2, place % 2
    at = jnp.where(chip == 0, 0, jnp.where(chip == 1, 4, jnp.where(chip == 2, 5, 1)))
    rows = load_images(block_ref, (at, at + 2), spread)
    half = [jnp.where(core == 0, ORDER[n], ORDER[n + 4]) for n in range(4)]
    columns = load_images(block_ref, half, spread, 2)
    tile, row_maps = pair_tile(rows, columns, weights_ref[...])
    tile_ref[...] = tile
    rows_ref[:, :3] = rows
    for layer in range(LAYERS):
        rows_ref[:, 3 + layer] = row_maps[layer][0]
        rows_ref[:, 6 + layer] = row_maps[layer][1]


def visitor_tile(rows_ref, block_ref, weights_ref, spread):
    columns = load_images(block_ref, ORDER, spread)
    row_maps = [(rows_ref[:, 3 + layer], rows_ref[:, 6 + layer]) for layer in range(LAYERS)]
    return pair_tile(rows_ref[:, :3], columns, weights_ref[...], row_maps)[0]


def visitor_kernel(rows_ref, block_ref, weights_ref, tile_ref, spread):
    tile_ref[...] = visitor_tile(rows_ref, block_ref, weights_ref, spread)


def last_kernel(rows_ref, block_ref, weights_ref, own_ref, inside_ref, tile_ref, spread):
    cross = visitor_tile(rows_ref, block_ref, weights_ref, spread)
    tile_ref[...] = own_ref[...] + pltpu.roll(inside_ref[...], 8, 1) + pltpu.roll(cross, 24, 1)


def assemble_kernel(both_ref, out_ref):
    level = lax.axis_index("blk") % 3
    core = lax.axis_index("grp") % 2
    low, high = [jnp.where(core == 0, both_ref[at, :2], both_ref[at, 2:4]) for at in (0, 1)]
    low_inside, high_inside = low[:, 8:24], high[:, 8:24]
    low_cross, high_cross = low[:, 24:40], high[:, 24:40]
    out_ref[0] = jnp.where(level == 2, low_inside, low_cross)
    out_ref[1] = jnp.where(level == 0, high_cross, high_inside)
    out_ref[2] = jnp.concatenate([low[:, :8], high[:, :8]], 1)
    out_ref[3] = jnp.where(level == 2, low_cross, low_inside)
    out_ref[4] = jnp.where(level == 0, high_inside, high_cross)


def call(body, outs, pairs, places):
    return pl.pallas_call(
        body,
        out_shape=outs,
        scratch_shapes=[pltpu.VMEM((places * 48, 128), jnp.float32)] if places else [],
        compiler_params=pltpu.CompilerParams(vmem_limit_bytes=32 * 1024 * 1024),
        cost_estimate=pl.CostEstimate(
            flops=pairs * 3 * 1024 * 512, bytes_accessed=1 << 20, transcendentals=pairs * 3 * 1024
        ),
    )


def routes():
    lines = 32

    def device(line, level, chip, core):
        return ((line % lines) * 3 + level) * GRP + chip * 2 + core

    across = {
        (0, 0): (-1, 1),
        (0, 1): (-1, 2),
        (1, 0): (-1, 2),
        (1, 1): (1, 0),
        (2, 0): (1, 0),
        (2, 1): (1, 1),
    }
    cross, inside, used = [], [], {}
    for line in range(lines):
        for chip in range(GRP // 2):
            for level in range(3):
                for core in (0, 1):
                    here = device(line, level, chip, core)
                    step, source = across[level, core]
                    sender = (line + step) % lines, source, chip
                    turn = used.get(sender, 0)
                    used[sender] = turn + 1
                    cross.append((device(*sender, turn), here))
                    source = (level + (2 if core else 1)) % 3
                    inside.append((device(line, source, chip, 1 - core), here))
    return cross, inside


def per_device(images):
    weights = jnp.asarray(stencil_weights(), jnp.bfloat16)
    mine = images.reshape(2, 3, 8, 128).transpose(1, 2, 0, 3).reshape(1, 48, 128)
    pairs = [[0, 6], [1, 7], [2, 4], [3, 5]]
    halves = [[0, 1, 2, 3], [6, 7, 4, 5]]
    block = lax.all_gather(mine, "grp", axis=0, tiled=True, axis_index_groups=pairs)
    block = lax.all_gather(block, "grp", axis=0, tiled=True, axis_index_groups=halves)
    cross_route, inside_route = routes()
    inside = lax.ppermute(block, ("blk", "grp"), inside_route)
    cross = lax.ppermute(block, ("blk", "grp"), cross_route)
    tile = jax.ShapeDtypeStruct((8, 128), jnp.float32)
    rows = jax.ShapeDtypeStruct((CHIP_ROWS, 9, 8, 128), jnp.float32)
    own_tile, row_maps = call(own_kernel, (tile, rows), 32, 6)(block, weights)
    inside_tile = call(visitor_kernel, tile, 64, GRP)(row_maps, inside, weights)
    packed = call(last_kernel, tile, 64, GRP)(row_maps, cross, weights, own_tile, inside_tile)
    chips = [[2 * chip, 2 * chip + 1] for chip in range(GRP // 2)]
    both = lax.all_gather(packed, "grp", axis=0, axis_index_groups=chips)
    result = call(assemble_kernel, jax.ShapeDtypeStruct((5, 2, 16), jnp.float32), 0, 0)(both)
    return jnp.transpose(result, (1, 0, 2))


def solution(mesh):
    in_specs = (P(("blk", "grp"), None, None),)
    out_specs = P(("blk", "grp"), None, None)
    return jax.shard_map(
        per_device, mesh=mesh, in_specs=in_specs, out_specs=out_specs, check_vma=False
    )
```

```python
import functools

import jax
import jax.numpy as jnp
import numpy as np
from jax import lax
from jax.experimental import pallas as pl
from jax.experimental.pallas import tpu as pltpu
from jax.sharding import PartitionSpec as P

SIDE = 32
LAYERS = 3
CHIP_ROWS = 4
GRP = 8
bias_var = 0.1

ORDER = (0, 2, 4, 6, 5, 7, 1, 3)

TAIL = (
    0.3001054023535799,
    0.015007729426877447,
    0.0023848543747712397,
    0.0006623160561359935,
    -2.0047167192458316e-05,
    0.00016959256815365074,
)


def stencil_weights():
    lane = np.arange(128)
    row, col = lane // SIDE, lane % SIDE
    near = np.abs(col[:, None] - col[None, :]) <= 1
    inner = near & (np.abs(row[:, None] - row[None, :]) <= 1)
    cross = near & (
        ((row[:, None] == 3) & (row[None, :] == 0)) | ((row[:, None] == 0) & (row[None, :] == 3))
    )
    half = np.concatenate([inner, cross], 1).astype(np.float32)
    return np.concatenate([half, half], 0)


def split(x):
    high = x.astype(jnp.bfloat16)
    low = (x - high.astype(jnp.float32)).astype(jnp.bfloat16)
    return high, low


def stencil_sum(maps, weights, from_above, from_below):
    count = maps.shape[0]
    high, low = split(maps.reshape(count * 8, 128))
    both = jnp.dot(
        jnp.concatenate([high, low], 1), weights, preferred_element_type=jnp.float32
    )
    inner = both[:, :128].reshape(count, 8, 128)
    cross = both[:, 128:].reshape(count, 8, 128)
    down = pltpu.roll(cross, 1, 1)
    up = pltpu.roll(cross, 7, 1)
    return inner + jnp.where(from_above, down, jnp.where(from_below, up, 0.0))


def masks():
    sub = lax.broadcasted_iota(jnp.int32, (1, 8, 128), 1)
    lane = lax.broadcasted_iota(jnp.int32, (1, 8, 128), 2)
    return (lane < SIDE) & (sub >= 1), (lane >= 3 * SIDE) & (sub <= 6)


def load_images(ref, places, spread, slot=0):
    images = []
    for place in places:
        spread[pl.ds(slot * 48, 48)] = ref[place].astype(jnp.float32)
        for image in range(2):
            images += [
                spread[pl.ds(slot * 48 + channel * 16 + image, 8, stride=2)]
                for channel in range(3)
            ]
        slot += 1
    return jnp.stack(images, 0).reshape(2 * len(places), 3, 8, 128)


def relu_over_scale(ratio):
    gap = 1.0 - jnp.minimum(jnp.abs(ratio), 1.0)
    poly = jnp.float32(TAIL[-1])
    for coefficient in TAIL[-2::-1]:
        poly = poly * gap + jnp.float32(coefficient)
    return jnp.clip(ratio, 0.0, 1.0) + gap * gap * lax.rsqrt(jnp.maximum(gap, 1e-30)) * poly


def fold(maps):
    sub = lax.broadcasted_iota(jnp.int32, (1, 8, 128), 1)
    for width in (4, 2, 1):
        first, second = maps[:width], maps[width:]
        low = (sub % (2 * width)) < width
        kept = jnp.where(low, first, second)
        if width == 4:
            other = pltpu.roll(jnp.where(low, second, first), 4, 1)
        else:
            other = jnp.where(low, pltpu.roll(first, 8 - width, 1), pltpu.roll(second, width, 1))
        maps = kept + other
    return maps[0]


def squares(channels):
    return jnp.sum(channels * channels, 1) * (1.0 / 27.0)


def pair_tile(row_channels, columns, weights, row_maps=None):
    above, below = masks()
    count = columns.shape[0]
    pairs = CHIP_ROWS * count
    maps = []
    for row in range(CHIP_ROWS):
        terms = (row_channels[row] * (1.0 / 27.0))[None] * columns
        maps.append(terms[:, 0] + terms[:, 1] + terms[:, 2])
    squared = squares(columns)
    if row_maps is None:
        squared = jnp.concatenate([squared, squares(row_channels)], 0)
    made = []
    for layer in range(LAYERS):
        variance = stencil_sum(squared, weights, above, below) + bias_var
        sums = stencil_sum(jnp.concatenate(maps, 0), weights, above, below) + bias_var
        inverse = lax.rsqrt(variance)
        scale = variance * inverse
        if row_maps is None:
            factor = 1.0 / 9.0 if layer < LAYERS - 1 else 1.0 / 1024.0
            row_inverse, row_scale = inverse[count:], scale[count:] * factor
            made.append((row_inverse, row_scale))
        else:
            row_inverse, row_scale = row_maps[layer]
        maps = []
        for row in range(CHIP_ROWS):
            part = sums[row * count : (row + 1) * count]
            ratio = part * (row_inverse[row][None] * inverse[:count])
            maps.append((row_scale[row][None] * scale[:count]) * relu_over_scale(ratio))
        squared = variance * (1.0 / 9.0)
    sub = lax.broadcasted_iota(jnp.int32, (8, 128), 0)
    lane = lax.broadcasted_iota(jnp.int32, (8, 128), 1)
    spots = []
    for row in range(CHIP_ROWS):
        spot = jnp.zeros((8, 128), jnp.float32)
        for group in range(0, count, 8):
            total = jnp.sum(fold(maps[row][group : group + 8]), 1, keepdims=True)
            spot = jnp.where(lane == sub + group, total, spot)
        spots.append(spot)
    spots += [jnp.zeros((8, 128), jnp.float32)] * (8 - CHIP_ROWS)
    tile = fold(jnp.stack(spots, 0))
    return tile, made


def own_kernel(block_ref, weights_ref, tile_ref, rows_ref, spread):
    place = lax.axis_index("grp")
    chip, core = place // 2, place % 2
    at = jnp.where(chip == 0, 0, jnp.where(chip == 1, 4, jnp.where(chip == 2, 5, 1)))
    rows = load_images(block_ref, (at, at + 2), spread)
    half = [jnp.where(core == 0, ORDER[n], ORDER[n + 4]) for n in range(4)]
    columns = load_images(block_ref, half, spread, 2)
    tile, row_maps = pair_tile(rows, columns, weights_ref[...])
    tile_ref[...] = tile
    rows_ref[:, :3] = rows
    for layer in range(LAYERS):
        rows_ref[:, 3 + layer] = row_maps[layer][0]
        rows_ref[:, 6 + layer] = row_maps[layer][1]


def visitor_tile(rows_ref, block_ref, weights_ref, spread):
    columns = load_images(block_ref, ORDER, spread)
    row_maps = [(rows_ref[:, 3 + layer], rows_ref[:, 6 + layer]) for layer in range(LAYERS)]
    return pair_tile(rows_ref[:, :3], columns, weights_ref[...], row_maps)[0]


def visitor_kernel(rows_ref, block_ref, weights_ref, tile_ref, spread):
    tile_ref[...] = visitor_tile(rows_ref, block_ref, weights_ref, spread)


def last_kernel(rows_ref, block_ref, weights_ref, own_ref, before_ref, tile_ref, spread):
    after = visitor_tile(rows_ref, block_ref, weights_ref, spread)
    tile_ref[...] = own_ref[...] + pltpu.roll(before_ref[...], 8, 1) + pltpu.roll(after, 24, 1)


def assemble_kernel(both_ref, out_ref):
    core = lax.axis_index("grp") % 2
    low, high = [jnp.where(core == 0, both_ref[at, :2], both_ref[at, 2:4]) for at in (0, 1)]
    out_ref[0] = high[:, 8:24]
    out_ref[1] = low[:, 8:24]
    out_ref[2] = jnp.concatenate([low[:, :8], high[:, :8]], 1)
    out_ref[3] = low[:, 24:40]
    out_ref[4] = high[:, 24:40]


def call(body, outs, pairs, places):
    return pl.pallas_call(
        body,
        out_shape=outs,
        scratch_shapes=[pltpu.VMEM((places * 48, 128), jnp.float32)] if places else [],
        compiler_params=pltpu.CompilerParams(vmem_limit_bytes=32 * 1024 * 1024),
        cost_estimate=pl.CostEstimate(
            flops=pairs * 3 * 1024 * 512, bytes_accessed=1 << 20, transcendentals=pairs * 3 * 1024
        ),
    )


def by_core(block, direction, blocks):
    route = []
    for block_index in range(blocks):
        for place in range(GRP):
            source = (block_index + direction * (place % 2 + 1)) % blocks
            route.append((source * GRP + place, block_index * GRP + place))
    return lax.ppermute(block, ("blk", "grp"), route)


def per_device(images):
    weights = jnp.asarray(stencil_weights(), jnp.bfloat16)
    mine = images.reshape(2, 3, 8, 128).transpose(1, 2, 0, 3).reshape(1, 48, 128)
    pairs = [[0, 6], [1, 7], [2, 4], [3, 5]]
    halves = [[0, 1, 2, 3], [6, 7, 4, 5]]
    block = lax.all_gather(mine, "grp", axis=0, tiled=True, axis_index_groups=pairs)
    block = lax.all_gather(block, "grp", axis=0, tiled=True, axis_index_groups=halves)
    blocks = lax.axis_size("blk")
    before = by_core(block, -1, blocks)
    after = by_core(block, 1, blocks)
    tile = jax.ShapeDtypeStruct((8, 128), jnp.float32)
    rows = jax.ShapeDtypeStruct((CHIP_ROWS, 9, 8, 128), jnp.float32)
    own_tile, row_maps = call(own_kernel, (tile, rows), 32, 6)(block, weights)
    before_tile = call(visitor_kernel, tile, 64, GRP)(row_maps, before, weights)
    packed = call(last_kernel, tile, 64, GRP)(row_maps, after, weights, own_tile, before_tile)
    chips = [[2 * chip, 2 * chip + 1] for chip in range(GRP // 2)]
    both = lax.all_gather(packed, "grp", axis=0, axis_index_groups=chips)
    result = call(assemble_kernel, jax.ShapeDtypeStruct((5, 2, 16), jnp.float32), 0, 0)(both)
    return jnp.transpose(result, (1, 0, 2))


def solution(mesh):
    in_specs = (P(("blk", "grp"), None, None),)
    out_specs = P(("blk", "grp"), None, None)
    return jax.shard_map(
        per_device, mesh=mesh, in_specs=in_specs, out_specs=out_specs, check_vma=False
    )
```

```python
import functools

import jax
import jax.numpy as jnp
import numpy as np
from jax import lax
from jax.experimental import pallas as pl
from jax.experimental.pallas import tpu as pltpu
from jax.sharding import PartitionSpec as P

SIDE = 32
LAYERS = 3
CHIP_ROWS = 4
GRP = 8
bias_var = 0.1

ORDER = (0, 2, 4, 6, 5, 7, 1, 3)

TAIL = (
    0.3001054023535799,
    0.015007729426877447,
    0.0023848543747712397,
    0.0006623160561359935,
    -2.0047167192458316e-05,
    0.00016959256815365074,
)


def stencil_weights():
    lane = np.arange(128)
    row, col = lane // SIDE, lane % SIDE
    near = np.abs(col[:, None] - col[None, :]) <= 1
    inner = near & (np.abs(row[:, None] - row[None, :]) <= 1)
    cross = near & (
        ((row[:, None] == 3) & (row[None, :] == 0)) | ((row[:, None] == 0) & (row[None, :] == 3))
    )
    half = np.concatenate([inner, cross], 1).astype(np.float32)
    return np.concatenate([half, half], 0)


def split(x):
    high = x.astype(jnp.bfloat16)
    low = (x - high.astype(jnp.float32)).astype(jnp.bfloat16)
    return high, low


def stencil_sum(maps, weights, from_above, from_below):
    count = maps.shape[0]
    high, low = split(maps.reshape(count * 8, 128))
    both = jnp.dot(
        jnp.concatenate([high, low], 1), weights, preferred_element_type=jnp.float32
    )
    inner = both[:, :128].reshape(count, 8, 128)
    cross = both[:, 128:].reshape(count, 8, 128)
    down = pltpu.roll(cross, 1, 1)
    up = pltpu.roll(cross, 7, 1)
    return inner + jnp.where(from_above, down, jnp.where(from_below, up, 0.0))


def masks():
    sub = lax.broadcasted_iota(jnp.int32, (1, 8, 128), 1)
    lane = lax.broadcasted_iota(jnp.int32, (1, 8, 128), 2)
    return (lane < SIDE) & (sub >= 1), (lane >= 3 * SIDE) & (sub <= 6)


def load_images(ref, places, spread, slot=0):
    images = []
    for place in places:
        spread[pl.ds(slot * 48, 48)] = ref[place].astype(jnp.float32)
        for image in range(2):
            images += [
                spread[pl.ds(slot * 48 + channel * 16 + image, 8, stride=2)]
                for channel in range(3)
            ]
        slot += 1
    return jnp.stack(images, 0).reshape(2 * len(places), 3, 8, 128)


def relu_over_scale(ratio):
    gap = jnp.maximum(1.0 - jnp.abs(ratio), 1e-30)
    poly = jnp.float32(TAIL[-1])
    for coefficient in TAIL[-2::-1]:
        poly = poly * gap + jnp.float32(coefficient)
    return jnp.clip(ratio, 0.0, 1.0) + gap * gap * lax.rsqrt(gap) * poly


def fold(maps):
    sub = lax.broadcasted_iota(jnp.int32, (1, 8, 128), 1)
    for width in (4, 2, 1):
        first, second = maps[:width], maps[width:]
        low = (sub % (2 * width)) < width
        kept = jnp.where(low, first, second)
        if width == 4:
            other = pltpu.roll(jnp.where(low, second, first), 4, 1)
        else:
            other = jnp.where(low, pltpu.roll(first, 8 - width, 1), pltpu.roll(second, width, 1))
        maps = kept + other
    return maps[0]


def squares(channels):
    return jnp.sum(channels * channels, 1) * (1.0 / 27.0)


def pair_tile(row_channels, columns, weights, row_maps=None):
    above, below = masks()
    count = columns.shape[0]
    pairs = CHIP_ROWS * count
    maps = []
    for row in range(CHIP_ROWS):
        terms = (row_channels[row] * (1.0 / 27.0))[None] * columns
        maps.append(terms[:, 0] + terms[:, 1] + terms[:, 2])
    squared = squares(columns)
    if row_maps is None:
        squared = jnp.concatenate([squared, squares(row_channels)], 0)
    made = []
    for layer in range(LAYERS):
        variance = stencil_sum(squared, weights, above, below) + bias_var
        inverse = lax.rsqrt(variance)
        scale = variance * inverse
        if row_maps is None:
            factor = 1.0 / 9.0 if layer < LAYERS - 1 else 1.0 / 1024.0
            row_inverse, row_scale = inverse[count:], scale[count:] * factor
            made.append((row_inverse, row_scale))
        else:
            row_inverse, row_scale = row_maps[layer]
        for row in range(CHIP_ROWS):
            cov = stencil_sum(maps[row], weights, above, below) + bias_var
            ratio = cov * (row_inverse[row][None] * inverse[:count])
            maps[row] = (row_scale[row][None] * scale[:count]) * relu_over_scale(ratio)
        squared = variance * (1.0 / 9.0)
    sub = lax.broadcasted_iota(jnp.int32, (8, 128), 0)
    lane = lax.broadcasted_iota(jnp.int32, (8, 128), 1)
    spots = []
    for row in range(CHIP_ROWS):
        spot = jnp.zeros((8, 128), jnp.float32)
        for group in range(0, count, 8):
            total = jnp.sum(fold(maps[row][group : group + 8]), 1, keepdims=True)
            spot = jnp.where(lane == sub + group, total, spot)
        spots.append(spot)
    spots += [jnp.zeros((8, 128), jnp.float32)] * (8 - CHIP_ROWS)
    tile = fold(jnp.stack(spots, 0))
    return tile, made


def own_kernel(block_ref, weights_ref, tile_ref, rows_ref, spread):
    place = lax.axis_index("grp")
    chip, core = place // 2, place % 2
    at = jnp.where(chip == 0, 0, jnp.where(chip == 1, 4, jnp.where(chip == 2, 5, 1)))
    rows = load_images(block_ref, (at, at + 2), spread)
    half = [jnp.where(core == 0, ORDER[n], ORDER[n + 4]) for n in range(4)]
    columns = load_images(block_ref, half, spread, 2)
    tile, row_maps = pair_tile(rows, columns, weights_ref[...])
    tile_ref[...] = tile
    rows_ref[:, :3] = rows
    for layer in range(LAYERS):
        rows_ref[:, 3 + layer] = row_maps[layer][0]
        rows_ref[:, 6 + layer] = row_maps[layer][1]


def visitor_tile(rows_ref, block_ref, weights_ref, spread):
    columns = load_images(block_ref, ORDER, spread)
    row_maps = [(rows_ref[:, 3 + layer], rows_ref[:, 6 + layer]) for layer in range(LAYERS)]
    return pair_tile(rows_ref[:, :3], columns, weights_ref[...], row_maps)[0]


def visitor_kernel(rows_ref, block_ref, weights_ref, tile_ref, spread):
    tile_ref[...] = visitor_tile(rows_ref, block_ref, weights_ref, spread)


def last_kernel(rows_ref, block_ref, weights_ref, own_ref, before_ref, tile_ref, spread):
    after = visitor_tile(rows_ref, block_ref, weights_ref, spread)
    tile_ref[...] = own_ref[...] + pltpu.roll(before_ref[...], 8, 1) + pltpu.roll(after, 24, 1)


def assemble_kernel(both_ref, out_ref):
    core = lax.axis_index("grp") % 2
    low, high = [jnp.where(core == 0, both_ref[at, :2], both_ref[at, 2:4]) for at in (0, 1)]
    out_ref[0] = low[:, 8:24]
    out_ref[1] = high[:, 8:24]
    out_ref[2] = jnp.concatenate([low[:, :8], high[:, :8]], 1)
    out_ref[3] = high[:, 24:40]
    out_ref[4] = low[:, 24:40]


def call(body, outs, pairs, places):
    return pl.pallas_call(
        body,
        out_shape=outs,
        scratch_shapes=[pltpu.VMEM((places * 48, 128), jnp.float32)] if places else [],
        compiler_params=pltpu.CompilerParams(vmem_limit_bytes=32 * 1024 * 1024),
        cost_estimate=pl.CostEstimate(
            flops=pairs * 3 * 1024 * 512, bytes_accessed=1 << 20, transcendentals=pairs * 3 * 1024
        ),
    )


def by_core(block, direction, nearer, blocks):
    route = []
    for block_index in range(blocks):
        for place in range(GRP):
            step = place % 2 + 1 if nearer else 2 - place % 2
            source = (block_index + direction * step) % blocks
            route.append((source * GRP + place, block_index * GRP + place))
    return lax.ppermute(block, ("blk", "grp"), route)


def per_device(images):
    weights = jnp.asarray(stencil_weights(), jnp.bfloat16)
    mine = images.reshape(2, 3, 8, 128).transpose(1, 2, 0, 3).reshape(1, 48, 128)
    pairs = [[0, 6], [1, 7], [2, 4], [3, 5]]
    halves = [[0, 1, 2, 3], [6, 7, 4, 5]]
    block = lax.all_gather(mine, "grp", axis=0, tiled=True, axis_index_groups=pairs)
    block = lax.all_gather(block, "grp", axis=0, tiled=True, axis_index_groups=halves)
    blocks = lax.axis_size("blk")
    before = by_core(block, -1, False, blocks)
    after = by_core(block, 1, False, blocks)
    tile = jax.ShapeDtypeStruct((8, 128), jnp.float32)
    rows = jax.ShapeDtypeStruct((CHIP_ROWS, 9, 8, 128), jnp.float32)
    own_tile, row_maps = call(own_kernel, (tile, rows), 32, 6)(block, weights)
    before_tile = call(visitor_kernel, tile, 64, GRP)(row_maps, before, weights)
    packed = call(last_kernel, tile, 64, GRP)(row_maps, after, weights, own_tile, before_tile)
    chips = [[2 * chip, 2 * chip + 1] for chip in range(GRP // 2)]
    both = lax.all_gather(packed, "grp", axis=0, axis_index_groups=chips)
    result = call(assemble_kernel, jax.ShapeDtypeStruct((5, 2, 16), jnp.float32), 0, 0)(both)
    return jnp.transpose(result, (1, 0, 2))


def solution(mesh):
    in_specs = (P(("blk", "grp"), None, None),)
    out_specs = P(("blk", "grp"), None, None)
    return jax.shard_map(
        per_device, mesh=mesh, in_specs=in_specs, out_specs=out_specs, check_vma=False
    )
```

```python
import functools

import jax
import jax.numpy as jnp
import numpy as np
from jax import lax
from jax.experimental import pallas as pl
from jax.experimental.pallas import tpu as pltpu
from jax.sharding import PartitionSpec as P

SIDE = 32
LAYERS = 3
CHIP_ROWS = 4
GRP = 8
bias_var = 0.1

ORDER = (0, 2, 4, 6, 5, 7, 1, 3)

TAIL = (
    0.3001054023535799,
    0.015007729426877447,
    0.0023848543747712397,
    0.0006623160561359935,
    -2.0047167192458316e-05,
    0.00016959256815365074,
)


def stencil_weights():
    lane = np.arange(128)
    row, col = lane // SIDE, lane % SIDE
    near = np.abs(col[:, None] - col[None, :]) <= 1
    inner = near & (np.abs(row[:, None] - row[None, :]) <= 1)
    cross = near & (
        ((row[:, None] == 3) & (row[None, :] == 0)) | ((row[:, None] == 0) & (row[None, :] == 3))
    )
    half = np.concatenate([inner, cross], 1).astype(np.float32)
    return np.concatenate([half, half], 0)


def split(x):
    high = x.astype(jnp.bfloat16)
    low = (x - high.astype(jnp.float32)).astype(jnp.bfloat16)
    return high, low


def stencil_sum(maps, weights, from_above, from_below):
    count = maps.shape[0]
    high, low = split(maps.reshape(count * 8, 128))
    both = jnp.dot(
        jnp.concatenate([high, low], 1), weights, preferred_element_type=jnp.float32
    )
    inner = both[:, :128].reshape(count, 8, 128)
    cross = both[:, 128:].reshape(count, 8, 128)
    down = pltpu.roll(cross, 1, 1)
    up = pltpu.roll(cross, 7, 1)
    return inner + jnp.where(from_above, down, jnp.where(from_below, up, 0.0))


def masks():
    sub = lax.broadcasted_iota(jnp.int32, (1, 8, 128), 1)
    lane = lax.broadcasted_iota(jnp.int32, (1, 8, 128), 2)
    return (lane < SIDE) & (sub >= 1), (lane >= 3 * SIDE) & (sub <= 6)


def load_images(ref, places, spread, slot=0):
    images = []
    for place in places:
        spread[pl.ds(slot * 48, 48)] = ref[place].astype(jnp.float32)
        for image in range(2):
            images += [
                spread[pl.ds(slot * 48 + channel * 16 + image, 8, stride=2)]
                for channel in range(3)
            ]
        slot += 1
    return jnp.stack(images, 0).reshape(2 * len(places), 3, 8, 128)


def relu_over_scale(ratio):
    gap = jnp.maximum(1.0 - jnp.abs(ratio), 1e-30)
    poly = jnp.float32(TAIL[-1])
    for coefficient in TAIL[-2::-1]:
        poly = poly * gap + jnp.float32(coefficient)
    return jnp.clip(ratio, 0.0, 1.0) + gap * gap * lax.rsqrt(gap) * poly


def fold(maps):
    sub = lax.broadcasted_iota(jnp.int32, (1, 8, 128), 1)
    for width in (4, 2, 1):
        first, second = maps[:width], maps[width:]
        low = (sub % (2 * width)) < width
        kept = jnp.where(low, first, second)
        if width == 4:
            other = pltpu.roll(jnp.where(low, second, first), 4, 1)
        else:
            other = jnp.where(low, pltpu.roll(first, 8 - width, 1), pltpu.roll(second, width, 1))
        maps = kept + other
    return maps[0]


def squares(channels):
    return jnp.sum(channels * channels, 1) * (1.0 / 27.0)


def pair_tile(row_channels, columns, weights, row_maps=None):
    above, below = masks()
    count = columns.shape[0]
    pairs = CHIP_ROWS * count
    maps = []
    for row in range(CHIP_ROWS):
        terms = (row_channels[row] * (1.0 / 27.0))[None] * columns
        maps.append(terms[:, 0] + terms[:, 1] + terms[:, 2])
    squared = squares(columns)
    if row_maps is None:
        squared = jnp.concatenate([squared, squares(row_channels)], 0)
    made = []
    for layer in range(LAYERS):
        variance = stencil_sum(squared, weights, above, below) + bias_var
        inverse = lax.rsqrt(variance)
        scale = variance * inverse
        if row_maps is None:
            factor = 1.0 / 9.0 if layer < LAYERS - 1 else 1.0 / 1024.0
            row_inverse, row_scale = inverse[count:], scale[count:] * factor
            made.append((row_inverse, row_scale))
        else:
            row_inverse, row_scale = row_maps[layer]
        for row in range(CHIP_ROWS):
            cov = stencil_sum(maps[row], weights, above, below) + bias_var
            ratio = cov * (row_inverse[row][None] * inverse[:count])
            maps[row] = (row_scale[row][None] * scale[:count]) * relu_over_scale(ratio)
        squared = variance * (1.0 / 9.0)
    sub = lax.broadcasted_iota(jnp.int32, (8, 128), 0)
    lane = lax.broadcasted_iota(jnp.int32, (8, 128), 1)
    spots = []
    for row in range(CHIP_ROWS):
        spot = jnp.zeros((8, 128), jnp.float32)
        for group in range(0, count, 8):
            total = jnp.sum(fold(maps[row][group : group + 8]), 1, keepdims=True)
            spot = jnp.where(lane == sub + group, total, spot)
        spots.append(spot)
    spots += [jnp.zeros((8, 128), jnp.float32)] * (8 - CHIP_ROWS)
    tile = fold(jnp.stack(spots, 0))
    return tile, made


def own_kernel(block_ref, weights_ref, tile_ref, rows_ref, spread):
    place = lax.axis_index("grp")
    chip, core = place // 2, place % 2
    at = jnp.where(chip == 0, 0, jnp.where(chip == 1, 4, jnp.where(chip == 2, 5, 1)))
    rows = load_images(block_ref, (at, at + 2), spread)
    half = [jnp.where(core == 0, ORDER[n], ORDER[n + 4]) for n in range(4)]
    columns = load_images(block_ref, half, spread, 2)
    tile, row_maps = pair_tile(rows, columns, weights_ref[...])
    tile_ref[...] = tile
    rows_ref[:, :3] = rows
    for layer in range(LAYERS):
        rows_ref[:, 3 + layer] = row_maps[layer][0]
        rows_ref[:, 6 + layer] = row_maps[layer][1]


def visitor_tile(rows_ref, block_ref, weights_ref, spread):
    columns = load_images(block_ref, ORDER, spread)
    row_maps = [(rows_ref[:, 3 + layer], rows_ref[:, 6 + layer]) for layer in range(LAYERS)]
    return pair_tile(rows_ref[:, :3], columns, weights_ref[...], row_maps)[0]


def visitor_kernel(rows_ref, block_ref, weights_ref, tile_ref, spread):
    tile_ref[...] = visitor_tile(rows_ref, block_ref, weights_ref, spread)


def last_kernel(rows_ref, block_ref, weights_ref, own_ref, before_ref, tile_ref, spread):
    core = lax.axis_index("grp") % 2
    after = visitor_tile(rows_ref, block_ref, weights_ref, spread)[:CHIP_ROWS, :16]
    before = before_ref[:CHIP_ROWS, :16]
    own = own_ref[...]
    own = jnp.where(core == 0, own, pltpu.roll(own, 8, 1))[:CHIP_ROWS, :16]
    tile_ref[0] = jnp.where(core == 0, before, 0.0)
    tile_ref[1] = jnp.where(core == 0, 0.0, before)
    tile_ref[2] = own
    tile_ref[3] = jnp.where(core == 0, 0.0, after)
    tile_ref[4] = jnp.where(core == 0, after, 0.0)


def call(body, outs, pairs, places):
    return pl.pallas_call(
        body,
        out_shape=outs,
        scratch_shapes=[pltpu.VMEM((places * 48, 128), jnp.float32)] if places else [],
        compiler_params=pltpu.CompilerParams(vmem_limit_bytes=32 * 1024 * 1024),
        cost_estimate=pl.CostEstimate(
            flops=pairs * 3 * 1024 * 512, bytes_accessed=1 << 20, transcendentals=pairs * 3 * 1024
        ),
    )


def by_core(block, direction, nearer, blocks):
    route = []
    for block_index in range(blocks):
        for place in range(GRP):
            step = place % 2 + 1 if nearer else 2 - place % 2
            source = (block_index + direction * step) % blocks
            route.append((source * GRP + place, block_index * GRP + place))
    return lax.ppermute(block, ("blk", "grp"), route)


def per_device(images):
    weights = jnp.asarray(stencil_weights(), jnp.bfloat16)
    mine = images.reshape(2, 3, 8, 128).transpose(1, 2, 0, 3).reshape(1, 48, 128)
    pairs = [[0, 6], [1, 7], [2, 4], [3, 5]]
    halves = [[0, 1, 2, 3], [6, 7, 4, 5]]
    block = lax.all_gather(mine, "grp", axis=0, tiled=True, axis_index_groups=pairs)
    block = lax.all_gather(block, "grp", axis=0, tiled=True, axis_index_groups=halves)
    blocks = lax.axis_size("blk")
    before = by_core(block, -1, False, blocks)
    after = by_core(block, 1, False, blocks)
    tile = jax.ShapeDtypeStruct((8, 128), jnp.float32)
    rows = jax.ShapeDtypeStruct((CHIP_ROWS, 9, 8, 128), jnp.float32)
    own_tile, row_maps = call(own_kernel, (tile, rows), 32, 6)(block, weights)
    before_tile = call(visitor_kernel, tile, 64, GRP)(row_maps, before, weights)
    span = jax.ShapeDtypeStruct((5, CHIP_ROWS, 16), jnp.float32)
    packed = call(last_kernel, span, 64, GRP)(row_maps, after, weights, own_tile, before_tile)
    chips = [[2 * chip, 2 * chip + 1] for chip in range(GRP // 2)]
    both = lax.all_gather(packed, "grp", axis=0, axis_index_groups=chips)
    first = lax.axis_index("grp") % 2 == 0
    result = jnp.where(first, both[0, :, :2] + both[1, :, :2], both[0, :, 2:] + both[1, :, 2:])
    return jnp.transpose(result, (1, 0, 2))


def solution(mesh):
    in_specs = (P(("blk", "grp"), None, None),)
    out_specs = P(("blk", "grp"), None, None)
    return jax.shard_map(
        per_device, mesh=mesh, in_specs=in_specs, out_specs=out_specs, check_vma=False
    )
```

```python
import functools

import jax
import jax.numpy as jnp
import numpy as np
from jax import lax
from jax.experimental import pallas as pl
from jax.experimental.pallas import tpu as pltpu
from jax.sharding import PartitionSpec as P

SIDE = 32
LAYERS = 3
CHIP_ROWS = 4
GRP = 8
bias_var = 0.1

ORDER = (0, 2, 4, 6, 5, 7, 1, 3)

TAIL = (
    0.3001054023535799,
    0.015007729426877447,
    0.0023848543747712397,
    0.0006623160561359935,
    -2.0047167192458316e-05,
    0.00016959256815365074,
)


def stencil_weights():
    lane = np.arange(128)
    row, col = lane // SIDE, lane % SIDE
    near = np.abs(col[:, None] - col[None, :]) <= 1
    inner = near & (np.abs(row[:, None] - row[None, :]) <= 1)
    cross = near & (
        ((row[:, None] == 3) & (row[None, :] == 0)) | ((row[:, None] == 0) & (row[None, :] == 3))
    )
    half = np.concatenate([inner, cross], 1).astype(np.float32)
    return np.concatenate([half, half], 0)


def split(x):
    high = x.astype(jnp.bfloat16)
    low = (x - high.astype(jnp.float32)).astype(jnp.bfloat16)
    return high, low


def stencil_sum(maps, weights, from_above, from_below):
    count = maps.shape[0]
    high, low = split(maps.reshape(count * 8, 128))
    both = jnp.dot(
        jnp.concatenate([high, low], 1), weights, preferred_element_type=jnp.float32
    )
    inner = both[:, :128].reshape(count, 8, 128)
    cross = both[:, 128:].reshape(count, 8, 128)
    down = pltpu.roll(cross, 1, 1)
    up = pltpu.roll(cross, 7, 1)
    return inner + jnp.where(from_above, down, jnp.where(from_below, up, 0.0))


def masks():
    sub = lax.broadcasted_iota(jnp.int32, (1, 8, 128), 1)
    lane = lax.broadcasted_iota(jnp.int32, (1, 8, 128), 2)
    return (lane < SIDE) & (sub >= 1), (lane >= 3 * SIDE) & (sub <= 6)


def load_images(ref, places, spread, slot=0):
    images = []
    for place in places:
        spread[pl.ds(slot * 48, 48)] = ref[place].astype(jnp.float32)
        for image in range(2):
            images += [
                spread[pl.ds(slot * 48 + channel * 16 + image, 8, stride=2)]
                for channel in range(3)
            ]
        slot += 1
    return jnp.stack(images, 0).reshape(2 * len(places), 3, 8, 128)


def relu_over_scale(ratio):
    gap = jnp.maximum(1.0 - jnp.abs(ratio), 1e-30)
    poly = jnp.float32(TAIL[-1])
    for coefficient in TAIL[-2::-1]:
        poly = poly * gap + jnp.float32(coefficient)
    return jnp.clip(ratio, 0.0, 1.0) + gap * gap * lax.rsqrt(gap) * poly


def fold(maps):
    sub = lax.broadcasted_iota(jnp.int32, (1, 8, 128), 1)
    if maps.shape[0] == 4:
        maps = maps + pltpu.roll(maps, 4, 1)
    for width in (4, 2, 1)[8 // maps.shape[0] - 1 :]:
        first, second = maps[:width], maps[width:]
        low = (sub % (2 * width)) < width
        kept = jnp.where(low, first, second)
        if width == 4:
            other = pltpu.roll(jnp.where(low, second, first), 4, 1)
        else:
            other = jnp.where(low, pltpu.roll(first, 8 - width, 1), pltpu.roll(second, width, 1))
        maps = kept + other
    return maps[0]


def squares(channels):
    return jnp.sum(channels * channels, 1) * (1.0 / 27.0)


def pair_tile(row_channels, columns, weights, row_maps=None):
    above, below = masks()
    count = columns.shape[0]
    pairs = CHIP_ROWS * count
    maps = []
    for row in range(CHIP_ROWS):
        terms = row_channels[row][None] * columns
        maps.append(terms[:, 0] + terms[:, 1] + terms[:, 2])
    squared = squares(columns)
    if row_maps is None:
        squared = jnp.concatenate([squared, squares(row_channels) * 729.0], 0)
    made = []
    for layer in range(LAYERS):
        variance = stencil_sum(squared, weights, above, below) + bias_var
        inverse = lax.rsqrt(variance)
        scale = variance * inverse
        if row_maps is None:
            factor = 1.0 / 9.0 if layer < LAYERS - 1 else 1.0 / 1024.0
            row_inverse, row_scale = inverse[count:], scale[count:] * factor
            made.append((row_inverse, row_scale))
        else:
            row_inverse, row_scale = row_maps[layer]
        for row in range(CHIP_ROWS):
            cov = stencil_sum(maps[row], weights, above, below) + bias_var
            ratio = cov * (row_inverse[row][None] * inverse[:count])
            maps[row] = (row_scale[row][None] * scale[:count]) * relu_over_scale(ratio)
        squared = variance * (1.0 / 9.0)
    sub = lax.broadcasted_iota(jnp.int32, (8, 128), 0)
    lane = lax.broadcasted_iota(jnp.int32, (8, 128), 1)
    spots = []
    for row in range(CHIP_ROWS):
        spot = jnp.zeros((8, 128), jnp.float32)
        for group in range(0, count, 8):
            total = jnp.sum(fold(maps[row][group : group + 8]), 1, keepdims=True)
            spot = jnp.where(lane == sub + group, total, spot)
        spots.append(spot)
    tile = fold(jnp.stack(spots, 0))
    return tile, made


def own_kernel(block_ref, weights_ref, tile_ref, rows_ref, spread):
    place = lax.axis_index("grp")
    chip, core = place // 2, place % 2
    at = jnp.where(chip == 0, 0, jnp.where(chip == 1, 4, jnp.where(chip == 2, 5, 1)))
    rows = load_images(block_ref, (at, at + 2), spread) * (1.0 / 27.0)
    half = [jnp.where(core == 0, ORDER[n], ORDER[n + 4]) for n in range(4)]
    columns = load_images(block_ref, half, spread, 2)
    tile, row_maps = pair_tile(rows, columns, weights_ref[...])
    tile_ref[...] = tile
    rows_ref[:, :3] = rows
    for layer in range(LAYERS):
        rows_ref[:, 3 + layer] = row_maps[layer][0]
        rows_ref[:, 6 + layer] = row_maps[layer][1]


def visitor_tile(rows_ref, block_ref, weights_ref, spread):
    columns = load_images(block_ref, ORDER, spread)
    row_maps = [(rows_ref[:, 3 + layer], rows_ref[:, 6 + layer]) for layer in range(LAYERS)]
    return pair_tile(rows_ref[:, :3], columns, weights_ref[...], row_maps)[0]


def visitor_kernel(rows_ref, block_ref, weights_ref, tile_ref, spread):
    tile_ref[...] = visitor_tile(rows_ref, block_ref, weights_ref, spread)


def last_kernel(rows_ref, block_ref, weights_ref, own_ref, before_ref, tile_ref, spread):
    core = lax.axis_index("grp") % 2
    after = visitor_tile(rows_ref, block_ref, weights_ref, spread)[:CHIP_ROWS, :16]
    before = before_ref[:CHIP_ROWS, :16]
    own = own_ref[...]
    own = jnp.where(core == 0, own, pltpu.roll(own, 8, 1))[:CHIP_ROWS, :16]
    tile_ref[0] = jnp.where(core == 0, before, 0.0)
    tile_ref[1] = jnp.where(core == 0, 0.0, before)
    tile_ref[2] = own
    tile_ref[3] = jnp.where(core == 0, 0.0, after)
    tile_ref[4] = jnp.where(core == 0, after, 0.0)


def call(body, outs, pairs, places):
    return pl.pallas_call(
        body,
        out_shape=outs,
        scratch_shapes=[pltpu.VMEM((places * 48, 128), jnp.float32)] if places else [],
        compiler_params=pltpu.CompilerParams(vmem_limit_bytes=32 * 1024 * 1024),
        cost_estimate=pl.CostEstimate(
            flops=pairs * 3 * 1024 * 512, bytes_accessed=1 << 20, transcendentals=pairs * 3 * 1024
        ),
    )


def by_core(block, direction, nearer, blocks):
    route = []
    for block_index in range(blocks):
        for place in range(GRP):
            step = place % 2 + 1 if nearer else 2 - place % 2
            source = (block_index + direction * step) % blocks
            route.append((source * GRP + place, block_index * GRP + place))
    return lax.ppermute(block, ("blk", "grp"), route)


def per_device(images):
    weights = jnp.asarray(stencil_weights(), jnp.bfloat16)
    mine = images.reshape(2, 3, 8, 128).transpose(1, 2, 0, 3).reshape(1, 48, 128)
    pairs = [[0, 6], [1, 7], [2, 4], [3, 5]]
    halves = [[0, 1, 2, 3], [6, 7, 4, 5]]
    block = lax.all_gather(mine, "grp", axis=0, tiled=True, axis_index_groups=pairs)
    block = lax.all_gather(block, "grp", axis=0, tiled=True, axis_index_groups=halves)
    blocks = lax.axis_size("blk")
    before = by_core(block, -1, False, blocks)
    after = by_core(block, 1, False, blocks)
    tile = jax.ShapeDtypeStruct((8, 128), jnp.float32)
    rows = jax.ShapeDtypeStruct((CHIP_ROWS, 9, 8, 128), jnp.float32)
    own_tile, row_maps = call(own_kernel, (tile, rows), 32, 6)(block, weights)
    before_tile = call(visitor_kernel, tile, 64, GRP)(row_maps, before, weights)
    span = jax.ShapeDtypeStruct((5, CHIP_ROWS, 16), jnp.float32)
    packed = call(last_kernel, span, 64, GRP)(row_maps, after, weights, own_tile, before_tile)
    chips = [[2 * chip, 2 * chip + 1] for chip in range(GRP // 2)]
    both = lax.all_gather(packed, "grp", axis=0, axis_index_groups=chips)
    first = lax.axis_index("grp") % 2 == 0
    result = jnp.where(first, both[0, :, :2] + both[1, :, :2], both[0, :, 2:] + both[1, :, 2:])
    return jnp.transpose(result, (1, 0, 2))


def solution(mesh):
    in_specs = (P(("blk", "grp"), None, None),)
    out_specs = P(("blk", "grp"), None, None)
    return jax.shard_map(
        per_device, mesh=mesh, in_specs=in_specs, out_specs=out_specs, check_vma=False
    )
```

```python
import functools

import jax
import jax.numpy as jnp
import numpy as np
from jax import lax
from jax.experimental import pallas as pl
from jax.experimental.pallas import tpu as pltpu
from jax.sharding import PartitionSpec as P

SIDE = 32
LAYERS = 3
CHIP_ROWS = 4
GRP = 8
bias_var = 0.1

ORDER = (0, 2, 4, 6, 5, 7, 1, 3)

TAIL = (
    0.3001054023535799,
    0.015007729426877447,
    0.0023848543747712397,
    0.0006623160561359935,
    -2.0047167192458316e-05,
    0.00016959256815365074,
)


def stencil_weights():
    lane = np.arange(128)
    row, col = lane // SIDE, lane % SIDE
    near = np.abs(col[:, None] - col[None, :]) <= 1
    inner = near & (np.abs(row[:, None] - row[None, :]) <= 1)
    cross = near & (
        ((row[:, None] == 3) & (row[None, :] == 0)) | ((row[:, None] == 0) & (row[None, :] == 3))
    )
    half = np.concatenate([inner, cross], 1).astype(np.float32)
    return np.concatenate([half, half], 0)


def split(x):
    high = x.astype(jnp.bfloat16)
    low = (x - high.astype(jnp.float32)).astype(jnp.bfloat16)
    return high, low


def stencil_sum(maps, weights, from_above, from_below):
    count = maps.shape[0]
    high, low = split(maps.reshape(count * 8, 128))
    both = jnp.dot(
        jnp.concatenate([high, low], 1), weights, preferred_element_type=jnp.float32
    )
    inner = both[:, :128].reshape(count, 8, 128)
    cross = both[:, 128:].reshape(count, 8, 128)
    down = pltpu.roll(cross, 1, 1)
    up = pltpu.roll(cross, 7, 1)
    return inner + jnp.where(from_above, down, jnp.where(from_below, up, 0.0))


def masks():
    sub = lax.broadcasted_iota(jnp.int32, (1, 8, 128), 1)
    lane = lax.broadcasted_iota(jnp.int32, (1, 8, 128), 2)
    return (lane < SIDE) & (sub >= 1), (lane >= 3 * SIDE) & (sub <= 6)


def load_images(ref, places, spread, slot=0):
    images = []
    for place in places:
        spread[pl.ds(slot * 48, 48)] = ref[place].astype(jnp.float32)
        for image in range(2):
            images += [
                spread[pl.ds(slot * 48 + channel * 16 + image, 8, stride=2)]
                for channel in range(3)
            ]
        slot += 1
    return jnp.stack(images, 0).reshape(2 * len(places), 3, 8, 128)


def relu_over_scale(ratio):
    gap = jnp.maximum(1.0 - jnp.abs(ratio), 1e-30)
    poly = jnp.float32(TAIL[-1])
    for coefficient in TAIL[-2::-1]:
        poly = poly * gap + jnp.float32(coefficient)
    return jnp.clip(ratio, 0.0, 1.0) + gap * gap * lax.rsqrt(gap) * poly


def fold(maps):
    sub = lax.broadcasted_iota(jnp.int32, (1, 8, 128), 1)
    if maps.shape[0] == 4:
        maps = maps + pltpu.roll(maps, 4, 1)
    for width in (4, 2, 1)[8 // maps.shape[0] - 1 :]:
        first, second = maps[:width], maps[width:]
        low = (sub % (2 * width)) < width
        kept = jnp.where(low, first, second)
        if width == 4:
            other = pltpu.roll(jnp.where(low, second, first), 4, 1)
        else:
            other = jnp.where(low, pltpu.roll(first, 8 - width, 1), pltpu.roll(second, width, 1))
        maps = kept + other
    return maps[0]


def squares(channels):
    return jnp.sum(channels * channels, 1) * (1.0 / 27.0)


def pair_tile(row_channels, columns, weights, row_maps=None):
    above, below = masks()
    count = columns.shape[0]
    pairs = CHIP_ROWS * count
    maps = []
    for row in range(CHIP_ROWS):
        terms = row_channels[row][None] * columns
        maps.append(terms[:, 0] + terms[:, 1] + terms[:, 2])
    squared = squares(columns)
    if row_maps is None:
        squared = jnp.concatenate([squared, squares(row_channels) * 729.0], 0)
    made = []
    for layer in range(LAYERS):
        variance = stencil_sum(squared, weights, above, below) + bias_var
        inverse = lax.rsqrt(variance)
        scale = variance * inverse
        if row_maps is None:
            factor = 1.0 / 9.0 if layer < LAYERS - 1 else 1.0 / 1024.0
            row_inverse, row_scale = inverse[count:], scale[count:] * factor
            made.append((row_inverse, row_scale))
        else:
            row_inverse, row_scale = row_maps[layer]
        for row in range(CHIP_ROWS):
            cov = stencil_sum(maps[row], weights, above, below) + bias_var
            ratio = cov * (row_inverse[row][None] * inverse[:count])
            maps[row] = (row_scale[row][None] * scale[:count]) * relu_over_scale(ratio)
        squared = variance * (1.0 / 9.0)
    sub = lax.broadcasted_iota(jnp.int32, (8, 128), 0)
    lane = lax.broadcasted_iota(jnp.int32, (8, 128), 1)
    spots = []
    for row in range(CHIP_ROWS):
        spot = jnp.zeros((8, 128), jnp.float32)
        for group in range(0, count, 8):
            total = jnp.sum(fold(maps[row][group : group + 8]), 1, keepdims=True)
            spot = jnp.where(lane == sub + group, total, spot)
        spots.append(spot)
    tile = fold(jnp.stack(spots, 0))
    return tile, made


def own_kernel(block_ref, weights_ref, tile_ref, rows_ref, spread):
    place = lax.axis_index("grp")
    chip, core = place // 2, place % 2
    at = jnp.where(chip == 0, 0, jnp.where(chip == 1, 4, jnp.where(chip == 2, 5, 1)))
    rows = load_images(block_ref, (at, at + 2), spread) * (1.0 / 27.0)
    half = [jnp.where(core == 0, ORDER[n], ORDER[n + 4]) for n in range(4)]
    columns = load_images(block_ref, half, spread, 2)
    tile, row_maps = pair_tile(rows, columns, weights_ref[...])
    tile_ref[...] = tile
    rows_ref[:, :3] = rows
    for layer in range(LAYERS):
        rows_ref[:, 3 + layer] = row_maps[layer][0]
        rows_ref[:, 6 + layer] = row_maps[layer][1]


def visitor_tile(rows_ref, block_ref, weights_ref, spread):
    columns = load_images(block_ref, ORDER, spread)
    row_maps = [(rows_ref[:, 3 + layer], rows_ref[:, 6 + layer]) for layer in range(LAYERS)]
    return pair_tile(rows_ref[:, :3], columns, weights_ref[...], row_maps)[0]


def visitor_kernel(rows_ref, block_ref, weights_ref, tile_ref, spread):
    tile_ref[...] = visitor_tile(rows_ref, block_ref, weights_ref, spread)


def last_kernel(rows_ref, block_ref, weights_ref, own_ref, before_ref, tile_ref, spread):
    core = lax.axis_index("grp") % 2
    after = visitor_tile(rows_ref, block_ref, weights_ref, spread)[:CHIP_ROWS, :16]
    before = before_ref[:CHIP_ROWS, :16]
    own = own_ref[...]
    own = jnp.where(core == 0, own, pltpu.roll(own, 8, 1))[:CHIP_ROWS, :16]
    tile_ref[0] = jnp.where(core == 0, before, 0.0)
    tile_ref[1] = jnp.where(core == 0, 0.0, before)
    tile_ref[2] = own
    tile_ref[3] = jnp.where(core == 0, 0.0, after)
    tile_ref[4] = jnp.where(core == 0, after, 0.0)


def call(body, outs, pairs, places):
    return pl.pallas_call(
        body,
        out_shape=outs,
        scratch_shapes=[pltpu.VMEM((places * 48, 128), jnp.float32)] if places else [],
        compiler_params=pltpu.CompilerParams(vmem_limit_bytes=32 * 1024 * 1024),
        cost_estimate=pl.CostEstimate(
            flops=pairs * 3 * 1024 * 512, bytes_accessed=1 << 20, transcendentals=pairs * 3 * 1024
        ),
    )


def by_core(block, direction, nearer, blocks):
    route = []
    for block_index in range(blocks):
        for place in range(GRP):
            step = place % 2 + 1 if nearer else 2 - place % 2
            source = (block_index + direction * step) % blocks
            sender = place
            if direction > 0 and (block_index % 3, place) in ((2, 1), (1, 2)):
                sender = 3 - place
            route.append((source * GRP + sender, block_index * GRP + place))
    return lax.ppermute(block, ("blk", "grp"), route)


def per_device(images):
    weights = jnp.asarray(stencil_weights(), jnp.bfloat16)
    mine = images.reshape(2, 3, 8, 128).transpose(1, 2, 0, 3).reshape(1, 48, 128)
    pairs = [[0, 6], [1, 7], [2, 4], [3, 5]]
    halves = [[0, 1, 2, 3], [6, 7, 4, 5]]
    block = lax.all_gather(mine, "grp", axis=0, tiled=True, axis_index_groups=pairs)
    block = lax.all_gather(block, "grp", axis=0, tiled=True, axis_index_groups=halves)
    blocks = lax.axis_size("blk")
    before = by_core(block, -1, False, blocks)
    after = by_core(block, 1, False, blocks)
    tile = jax.ShapeDtypeStruct((8, 128), jnp.float32)
    rows = jax.ShapeDtypeStruct((CHIP_ROWS, 9, 8, 128), jnp.float32)
    own_tile, row_maps = call(own_kernel, (tile, rows), 32, 6)(block, weights)
    before_tile = call(visitor_kernel, tile, 64, GRP)(row_maps, before, weights)
    span = jax.ShapeDtypeStruct((5, CHIP_ROWS, 16), jnp.float32)
    packed = call(last_kernel, span, 64, GRP)(row_maps, after, weights, own_tile, before_tile)
    chips = [[2 * chip, 2 * chip + 1] for chip in range(GRP // 2)]
    both = lax.all_gather(packed, "grp", axis=0, axis_index_groups=chips)
    first = lax.axis_index("grp") % 2 == 0
    result = jnp.where(first, both[0, :, :2] + both[1, :, :2], both[0, :, 2:] + both[1, :, 2:])
    return jnp.transpose(result, (1, 0, 2))


def solution(mesh):
    in_specs = (P(("blk", "grp"), None, None),)
    out_specs = P(("blk", "grp"), None, None)
    return jax.shard_map(
        per_device, mesh=mesh, in_specs=in_specs, out_specs=out_specs, check_vma=False
    )
```
